32 devices in a mesh: row: 2 (over x), col: 4 (over z), depth: 4 (over y, core).
Axes of the slice: x: 2, y: 2, z: 4, core: 2. Of those that a mesh axis runs over, the one named last changes fastest.
Arguments:
- row_blocks: bfloat16 [32, 4, 6, 64, 64], P(('row', 'depth'), 'col'), may hold values from -1.5 to 1.5
- row_positions: int32 [32, 4, 6], P(('row', 'depth'), 'col'), may hold values from 0 to 11, as said below
- row_counts: int32 [32, 4], P(('row', 'depth'), 'col'), may hold values from 1 to 6, as said below
- col_blocks: bfloat16 [4, 128, 6, 64, 64], P('row', ('col', 'depth')), may hold values from -1.5 to 1.5
- col_positions: int32 [4, 128, 6], P('row', ('col', 'depth')), may hold values from 0 to 11, as said below
- col_counts: int32 [4, 128], P('row', ('col', 'depth')), may hold values from 1 to 6, as said below
Outputs:
- square: bfloat16 [2048, 8192], P('row', ('col', 'depth'))
The draws below stay inside these ranges and needn't reach their ends.
Inputs may be any that keep to these rules, and one draw needn't show every extreme that they name: `row_positions`: the positions listed for one block row and panel are distinct. `row_counts`: in every panel some block row lists exactly 6 blocks. `col_positions`: the positions listed for one block column and panel are distinct. `col_counts`: in every panel some block column lists exactly 6 blocks.
All inputs are finite; a program needn't handle non-finite values.
Results may differ from the reference program's by a relative error of at most 0.001.
Values may be sent and summed in bfloat16 or wider, within the bound.
A program may use at most 64 MiB of HBM per device.

```python
import jax
import jax.numpy as jnp

BS = 64
KP = 12
SPG = 6
G = 4
WROWS = 32
WCOLS = 128


def distinct_positions(key, lead_shape):
    scores = jax.random.randint(key, lead_shape + (KP,), 0, 2 ** 20) * KP + jnp.arange(KP, dtype=jnp.int32)
    return jnp.argsort(scores, axis=-1)[..., :SPG].astype(jnp.int32)


def draw_row_positions(key, part):
    return distinct_positions(key, (WROWS, G))


def draw_col_positions(key, part):
    return distinct_positions(key, (G, WCOLS))


def draw_row_counts(key, part):
    base_counts = jax.random.randint(key, (WROWS, G), 1, SPG + 1)
    chosen = jax.random.randint(jax.random.fold_in(key, 7), (G,), 0, WROWS)
    return base_counts.at[chosen, jnp.arange(G)].set(SPG).astype(jnp.int32)


def draw_col_counts(key, part):
    base_counts = jax.random.randint(key, (G, WCOLS), 1, SPG + 1)
    chosen = jax.random.randint(jax.random.fold_in(key, 11), (G,), 0, WCOLS)
    return base_counts.at[jnp.arange(G), chosen].set(SPG).astype(jnp.int32)


def levels(stream_key, dims, cuts, least, largest):
    gain, own = 1.0, jax.random.fold_in(stream_key, 6)
    for axis_at, shards_of in cuts:
        steps = jnp.exp(jax.random.uniform(jax.random.fold_in(own, axis_at), (shards_of,), jnp.float32, least / len(cuts), largest / len(cuts)))
        gain = gain * jnp.repeat(steps, dims[axis_at] // shards_of).reshape([-1 if axis == axis_at else 1 for axis in range(len(dims))])
    return gain


def bell_draw(key, extent, width, limit, shards=(), held_as=jnp.bfloat16):
    result = width * jax.random.normal(key, extent, jnp.float32)
    if shards:
        result = result * levels(key, extent, shards, -0.22, 0.18)
    return jnp.clip(result, -limit, limit).astype(held_as)


def setup_inputs(seed: int = 0) -> dict:
    splits = jax.random.split(jax.random.key(seed), 7)
    return {
        "row_blocks": bell_draw(splits[0], (WROWS, G, SPG, BS, BS), (4 * G) ** -0.5, 1.5, ((0, 8), (1, 4))),
        "row_positions": draw_row_positions(jax.random.fold_in(splits[6], 71), 0),
        "row_counts": draw_row_counts(jax.random.fold_in(splits[6], 71), 0),
        "col_blocks": bell_draw(splits[3], (G, WCOLS, SPG, BS, BS), (4 * G) ** -0.5, 1.5, ((0, 2), (1, 16))),
        "col_positions": draw_col_positions(jax.random.fold_in(splits[6], 71), 0),
        "col_counts": draw_col_counts(jax.random.fold_in(splits[6], 71), 0),
    }


def dense_rows(row_blocks, row_positions, row_counts):
    live_slot = jnp.arange(SPG, dtype=jnp.int32)[None, None, :] < row_counts[:, :, None]
    targets = jnp.arange(KP, dtype=jnp.int32)
    onehot = ((row_positions[:, :, :, None] == targets[None, None, None, :]) & live_slot[:, :, :, None]).astype(jnp.float32)
    spread = jnp.einsum("igsp,igsab->iagpb", onehot, row_blocks.astype(jnp.float32))
    return spread.reshape(WROWS * BS, G * KP * BS).astype(jnp.bfloat16)


def dense_cols(col_blocks, col_positions, col_counts):
    live_slot = jnp.arange(SPG, dtype=jnp.int32)[None, None, :] < col_counts[:, :, None]
    targets = jnp.arange(KP, dtype=jnp.int32)
    onehot = ((col_positions[:, :, :, None] == targets[None, None, None, :]) & live_slot[:, :, :, None]).astype(jnp.float32)
    spread = jnp.einsum("gjsp,gjsab->gpajb", onehot, col_blocks.astype(jnp.float32))
    return spread.reshape(G * KP * BS, WCOLS * BS).astype(jnp.bfloat16)


def reference(row_blocks, row_positions, row_counts, col_blocks, col_positions, col_counts):
    left_dense = dense_rows(row_blocks, row_positions, row_counts)
    right_dense = dense_cols(col_blocks, col_positions, col_counts)
    return jnp.dot(left_dense, right_dense, preferred_element_type=jnp.float32).astype(jnp.bfloat16)
```

```python
import functools

import jax
import jax.numpy as jnp
from jax import lax
from jax.experimental import pallas as pl
from jax.experimental.pallas import tpu as pltpu
from jax.sharding import PartitionSpec as P

KP = 12


def packed(blocks):
    *lead, side, _ = blocks.shape
    half = side // 2
    halves = blocks.reshape(-1, 2, half, side)
    return jnp.concatenate([halves[:, 0], halves[:, 1]], axis=-1)


def slot_table(positions, counts, first, dead):
    lists, slots = positions.shape
    slot = jnp.arange(slots, dtype=jnp.int32)
    live = slot[None, :] < counts[:, None]
    hit = (positions[:, :, None] == jnp.arange(KP, dtype=jnp.int32)[None, None, :]) & live[:, :, None]
    place = first + jnp.arange(lists, dtype=jnp.int32)[:, None] * slots + slot[None, :]
    found = jnp.sum(jnp.where(hit, place[:, :, None] + 1, 0), axis=1)
    return jnp.where(found > 0, found - 1, dead)


def side_by_side(a, b):
    half = a.shape[-1] // 2
    top = jnp.concatenate([a[:, :half], b[:, :half]], axis=1)
    bottom = jnp.concatenate([a[:, half:], b[:, half:]], axis=1)
    return top, bottom


def local_kernel(dims, left_tab, right_tab, left_hbm, right_hbm, out_ref, lbuf, rbuf, ld, rd, sems):
    cols, layers, rl, panels, cl, side = dims
    half = side // 2
    nl, nr = left_hbm.shape[0], right_hbm.shape[0]
    get_left = pltpu.make_async_copy(left_hbm, lbuf.at[pl.ds(0, nl)], sems.at[0])
    get_right = pltpu.make_async_copy(right_hbm, rbuf.at[pl.ds(0, nr)], sems.at[1])
    get_right.start()
    get_left.start()
    lbuf[nl] = jnp.zeros_like(lbuf[nl])
    rbuf[nr] = jnp.zeros_like(rbuf[nr])
    get_right.wait()

    def right_step(step, carry):
        g, p = step // KP, step % KP
        base = pl.multiple_of(step * side, side)
        for jp in range(cl // 2):
            a = rbuf[right_tab[(g * cl + 2 * jp) * KP + p]]
            b = rbuf[right_tab[(g * cl + 2 * jp + 1) * KP + p]]
            top, bottom = side_by_side(a, b)
            rd[pl.ds(base, half), jp * 2 * side : (jp + 1) * 2 * side] = top
            rd[pl.ds(base + half, half), jp * 2 * side : (jp + 1) * 2 * side] = bottom
        return carry

    lax.fori_loop(0, panels * KP, right_step, 0)
    get_left.wait()

    def left_step(row, carry):
        base = pl.multiple_of(row * side, side)
        d, i = row // rl, row % rl
        for c in range(cols):
            tab = ((c * layers + d) * rl + i) * KP
            for q in range(KP // 2):
                a = lbuf[left_tab[tab + 2 * q]]
                b = lbuf[left_tab[tab + 2 * q + 1]]
                top, bottom = side_by_side(a, b)
                at = (c * KP // 2 + q) * 2 * side
                ld[pl.ds(base, half), at : at + 2 * side] = top
                ld[pl.ds(base + half, half), at : at + 2 * side] = bottom
        return carry

    lax.fori_loop(0, layers * rl, left_step, 0)
    tile = 256

    def multiply(m, carry):
        at = pl.ds(pl.multiple_of(m * tile, tile), tile)
        out_ref[at, :] = jnp.dot(ld[at, :], rd[...], preferred_element_type=jnp.float32).astype(jnp.bfloat16)
        return carry

    lax.fori_loop(0, out_ref.shape[0] // tile, multiply, 0)


def on_device(row_blocks, row_positions, row_counts, col_blocks, col_positions, col_counts):
    rows, cols, layers = lax.axis_size("row"), lax.axis_size("col"), lax.axis_size("depth")
    rl, _, slots, side, _ = row_blocks.shape
    pg, cl = col_blocks.shape[:2]
    panels = pg * rows
    nl, nr = cols * layers * rl * slots, panels * cl * slots
    owner = lax.axis_index("col") * layers + lax.axis_index("depth")
    left_tab = slot_table(row_positions[:, 0], row_counts[:, 0], owner * rl * slots, nl)
    right_tab = slot_table(
        col_positions.reshape(pg * cl, slots), col_counts.reshape(pg * cl), lax.axis_index("row") * pg * cl * slots, nr
    )
    left = lax.all_gather(packed(row_blocks), ("col", "depth"), axis=0, tiled=True)
    right = lax.all_gather(packed(col_blocks), "row", axis=0, tiled=True)
    left_tab = lax.all_gather(left_tab.reshape(-1), ("col", "depth"), axis=0, tiled=True)
    right_tab = lax.all_gather(right_tab.reshape(-1), "row", axis=0, tiled=True)
    m, n, k = layers * rl * side, cl * side, panels * KP * side
    half = side // 2
    any_spec = pl.BlockSpec(memory_space=pl.ANY)
    return pl.pallas_call(
        functools.partial(local_kernel, (cols, layers, rl, panels, cl, side)),
        out_shape=jax.ShapeDtypeStruct((m, n), jnp.bfloat16),
        in_specs=[pl.BlockSpec(memory_space=pltpu.SMEM)] * 2 + [any_spec] * 2,
        out_specs=pl.BlockSpec(memory_space=pltpu.VMEM),
        scratch_shapes=[
            pltpu.VMEM((nl + 1, half, 2 * side), jnp.bfloat16),
            pltpu.VMEM((nr + 1, half, 2 * side), jnp.bfloat16),
            pltpu.VMEM((m, k), jnp.bfloat16),
            pltpu.VMEM((k, n), jnp.bfloat16),
            pltpu.SemaphoreType.DMA((2,)),
        ],
        compiler_params=pltpu.CompilerParams(vmem_limit_bytes=48 * 1024 * 1024),
        cost_estimate=pl.CostEstimate(flops=2 * m * n * k, bytes_accessed=2 * (m * n + (nl + nr) * side * side), transcendentals=0),
    )(left_tab, right_tab, left, right)


def solution(mesh):
    in_specs = (
        P(("row", "depth"), "col", None, None, None),
        P(("row", "depth"), "col", None),
        P(("row", "depth"), "col"),
        P("row", ("col", "depth"), None, None, None),
        P("row", ("col", "depth"), None),
        P("row", ("col", "depth")),
    )
    return jax.shard_map(
        on_device, mesh=mesh, in_specs=in_specs, out_specs=P("row", ("col", "depth")), check_vma=False
    )
```

```python
import functools

import jax
import jax.numpy as jnp
from jax import lax
from jax.experimental import pallas as pl
from jax.experimental.pallas import tpu as pltpu
from jax.sharding import PartitionSpec as P

KP = 12
MESH = pl.DeviceIdType.MESH
TAB = 16


def slot_table(positions, counts):
    slots = positions.shape[-1]
    slot = jnp.arange(slots, dtype=jnp.int32)
    live = slot < counts[..., None]
    hit = (positions[..., :, None] == jnp.arange(KP, dtype=jnp.int32)) & live[..., :, None]
    found = jnp.sum(jnp.where(hit, slot[:, None] + 1, 0), axis=-2)
    return found.astype(jnp.bfloat16)


def partner(index, bit):
    return index + bit - 2 * bit * ((index // bit) % 2)


def bits_of(size):
    bits = []
    while size > 1:
        size //= 2
        bits.append(size)
    return bits


def moved(index, e, bits):
    for bit in bits:
        if e & bit:
            index = partner(index, bit)
    return index


def lower_bits(e, bits):
    return [n for n, bit in enumerate(bits) if e == 0 or bit < (e & -e)]


def placed(tab, row, parts):
    want = jnp.broadcast_to(tab[row : row + 1, :], (TAB, tab.shape[1]))
    outs = [jnp.zeros_like(part) for part in parts[0]]
    for s, part in enumerate(parts):
        mask = want == jnp.asarray(s + 1, tab.dtype)
        outs = [jnp.where(mask, new, old) for new, old in zip(part, outs)]
    return outs


def kernel(dims, lblk, ltab, rblk, rtab, out_ref, lbuf, rbuf, ld, rd, lsend, lrecv, rsend, rrecv):
    rows, cols, layers, rl, pg, cl, slots, side = dims
    half = side // 2
    width = 2 * side
    r, c, d = lax.axis_index("row"), lax.axis_index("col"), lax.axis_index("depth")
    lbits, rbits = bits_of(layers), bits_of(rows)
    chunks = pg * cl // 2
    me = c * layers + d

    barrier = pltpu.get_barrier_semaphore()
    peers = [{"depth": partner(d, bit)} for bit in lbits] + [{"row": partner(r, bit)} for bit in rbits]
    if cols > 1:
        peers += [{"col": lax.rem(c + 1, cols)}, {"col": lax.rem(c + cols - 1, cols)}]
    for peer in peers:
        pl.semaphore_signal(barrier, inc=1, device_id=peer, device_id_type=MESH)

    def pack_left(i, carry):
        for s in range(slots):
            x = lblk[i, s]
            lbuf[me, i, s * half : (s + 1) * half, :] = jnp.concatenate([x[:half], x[half:]], axis=1)
        lbuf[me, i, slots * half : slots * half + TAB, :] = ltab[i]
        return carry

    lax.fori_loop(0, rl, pack_left, 0)
    pl.semaphore_wait(barrier, len(peers))

    def left_copy(way, owner, device):
        return pltpu.make_async_remote_copy(
            src_ref=lbuf.at[owner],
            dst_ref=lbuf.at[owner],
            send_sem=lsend.at[way, owner],
            recv_sem=lrecv.at[owner],
            device_id=device,
            device_id_type=MESH,
        )

    def left_sends(t, side_of, e, act):
        src = c + t if side_of else c - t
        owner = src * layers + moved(d, e, lbits)
        if e == 0:
            if side_of == 0:
                @pl.when(c + 1 < cols)
                def _():
                    act(left_copy(0, owner, {"col": c + 1}))

            def to_lower():
                act(left_copy(1, owner, {"col": c - 1}))

            if side_of == 1:
                pl.when(c > 0)(to_lower)
            else:
                pl.when((c > 0) & (t == 0))(to_lower)
        for n in lower_bits(e, lbits):
            act(left_copy(2 + n, owner, {"depth": partner(d, lbits[n])}))

    def valid(t, side_of):
        if side_of:
            return (t > 0) & (c + t < cols)
        return (t >= 0) & (c - t >= 0)

    left_sends(0, 0, 0, lambda copy: copy.start())

    def right_copy(n, owner, chunk):
        return pltpu.make_async_remote_copy(
            src_ref=rbuf.at[owner, chunk],
            dst_ref=rbuf.at[owner, chunk],
            send_sem=rsend.at[n, owner, chunk],
            recv_sem=rrecv.at[owner, chunk],
            device_id={"row": partner(r, rbits[n])},
            device_id_type=MESH,
        )

    def pack_right(chunk, carry):
        for s in range(slots):
            rbuf[r, chunk, s * side : (s + 1) * side, :] = jnp.concatenate(
                [rblk[2 * chunk, s], rblk[2 * chunk + 1, s]], axis=1
            )
        rbuf[r, chunk, slots * side : slots * side + TAB, :] = rtab[chunk]
        for n in lower_bits(0, rbits):
            right_copy(n, r, chunk).start()
        return carry

    lax.fori_loop(0, chunks, pack_right, 0)

    def place_right(owner, chunk):
        g = owner * pg + chunk // (cl // 2)
        lanes = pl.ds(pl.multiple_of((chunk % (cl // 2)) * width, width), width)
        tab = rbuf[owner, chunk, slots * side : slots * side + TAB, :]
        for v in range(side // TAB):
            parts = [(rbuf[owner, chunk, s * side + v * TAB : s * side + (v + 1) * TAB, :],) for s in range(slots)]
            for p in range(KP):
                (block,) = placed(tab, p, parts)
                rd[pl.ds(pl.multiple_of((g * KP + p) * side + v * TAB, TAB), TAB), lanes] = block

    def place_left(src, layer):
        owner = src * layers + layer

        def one(i, carry):
            base = (layer * rl + i) * side
            tab = lbuf[owner, i, slots * half : slots * half + TAB, :]
            for v in range(half // TAB):
                parts = []
                for s in range(slots):
                    x = lbuf[owner, i, s * half + v * TAB : s * half + (v + 1) * TAB, :]
                    lo, hi = x[:, :side], x[:, side:]
                    parts.append((jnp.concatenate([lo, lo], axis=1), jnp.concatenate([hi, hi], axis=1)))
                for q in range(KP // 2):
                    top, bottom = placed(tab, q, parts)
                    lanes = pl.ds(pl.multiple_of((src * (KP // 2) + q) * width, width), width)
                    ld[pl.ds(pl.multiple_of(base + v * TAB, TAB), TAB), lanes] = top
                    ld[pl.ds(pl.multiple_of(base + half + v * TAB, TAB), TAB), lanes] = bottom
            return carry

        lax.fori_loop(0, rl, one, 0)

    def own_right(chunk, carry):
        place_right(r, chunk)
        return carry

    lax.fori_loop(0, chunks, own_right, 0)

    order = sorted(range(layers), key=lambda e: (e.bit_count(), -e))
    last = max(e.bit_count() for e in order)

    def left_step(t, carry):
        for e in order:
            lag = e.bit_count()
            for side_of in (0, 1):
                tt = t - lag

                @pl.when(valid(tt, side_of) & (tt < cols))
                def _(tt=tt, e=e, side_of=side_of):
                    src = c + tt if side_of else c - tt
                    layer = moved(d, e, lbits)

                    def arrive():
                        left_copy(0, src * layers + layer, {"depth": partner(d, 1)}).wait_recv()
                        left_sends(tt, side_of, e, lambda copy: copy.start())

                    if e == 0:
                        pl.when(tt > 0)(arrive)
                    else:
                        arrive()
                    place_left(src, layer)
        return carry

    lax.fori_loop(0, cols + last, left_step, 0)

    for e in sorted(range(1, rows), key=lambda e: (e.bit_count(), -e)):
        owner = moved(r, e, rbits)

        def right_step(chunk, carry, owner=owner, e=e):
            right_copy(0, owner, chunk).wait_recv()
            for n in lower_bits(e, rbits):
                right_copy(n, owner, chunk).start()
            place_right(owner, chunk)
            return carry

        lax.fori_loop(0, chunks, right_step, 0)

    tile = 256

    def multiply(m, carry):
        at = pl.ds(pl.multiple_of(m * tile, tile), tile)
        out_ref[at, :] = jnp.dot(ld[at, :], rd[...], preferred_element_type=jnp.float32).astype(jnp.bfloat16)
        return carry

    lax.fori_loop(0, out_ref.shape[0] // tile, multiply, 0)

    def left_done(t, carry):
        for e in range(layers):
            for side_of in (0, 1):

                @pl.when(valid(t, side_of))
                def _(e=e, side_of=side_of):
                    left_sends(t, side_of, e, lambda copy: copy.wait_send())

        return carry

    lax.fori_loop(0, cols, left_done, 0)
    for e in range(rows):
        owner = moved(r, e, rbits)

        def right_done(chunk, carry, owner=owner, e=e):
            for n in lower_bits(e, rbits):
                right_copy(n, owner, chunk).wait_send()
            return carry

        lax.fori_loop(0, chunks, right_done, 0)


def lane_pairs(pairs, side):
    wide = jnp.repeat(pairs, side, axis=-1)
    return jnp.pad(wide, [(0, 0)] * (wide.ndim - 2) + [(0, TAB - wide.shape[-2]), (0, 0)])


def on_device(row_blocks, row_positions, row_counts, col_blocks, col_positions, col_counts):
    rows, cols, layers = lax.axis_size("row"), lax.axis_size("col"), lax.axis_size("depth")
    rl, _, slots, side, _ = row_blocks.shape
    pg, cl = col_blocks.shape[:2]
    panels = pg * rows
    chunks = pg * cl // 2
    left_tab = slot_table(row_positions[:, 0], row_counts[:, 0])
    left_tab = lane_pairs(left_tab.reshape(rl, KP // 2, 2), side)
    right_tab = slot_table(col_positions, col_counts).reshape(chunks, 2, KP)
    right_tab = lane_pairs(right_tab.transpose(0, 2, 1), side)
    m, n, k = layers * rl * side, cl * side, panels * KP * side
    width = 2 * side
    vmem = pl.BlockSpec(memory_space=pltpu.VMEM)
    return pl.pallas_call(
        functools.partial(kernel, (rows, cols, layers, rl, pg, cl, slots, side)),
        out_shape=jax.ShapeDtypeStruct((m, n), jnp.bfloat16),
        in_specs=[vmem] * 4,
        out_specs=vmem,
        scratch_shapes=[
            pltpu.VMEM((cols * layers, rl, slots * side // 2 + TAB, width), jnp.bfloat16),
            pltpu.VMEM((rows, chunks, slots * side + TAB, width), jnp.bfloat16),
            pltpu.VMEM((m, k), jnp.bfloat16),
            pltpu.VMEM((k, n), jnp.bfloat16),
            pltpu.SemaphoreType.DMA((2 + len(bits_of(layers)), cols * layers)),
            pltpu.SemaphoreType.DMA((cols * layers,)),
            pltpu.SemaphoreType.DMA((len(bits_of(rows)), rows, chunks)),
            pltpu.SemaphoreType.DMA((rows, chunks)),
        ],
        compiler_params=pltpu.CompilerParams(
            collective_id=0, has_side_effects=True, vmem_limit_bytes=48 * 1024 * 1024
        ),
        cost_estimate=pl.CostEstimate(flops=2 * m * n * k, bytes_accessed=2 * m * n, transcendentals=0),
    )(row_blocks[:, 0], left_tab, col_blocks.reshape(pg * cl, slots, side, side), right_tab)


def solution(mesh):
    in_specs = (
        P(("row", "depth"), "col", None, None, None),
        P(("row", "depth"), "col", None),
        P(("row", "depth"), "col"),
        P("row", ("col", "depth"), None, None, None),
        P("row", ("col", "depth"), None),
        P("row", ("col", "depth")),
    )
    return jax.shard_map(
        on_device, mesh=mesh, in_specs=in_specs, out_specs=P("row", ("col", "depth")), check_vma=False
    )
```

```python
import functools

import jax
import jax.numpy as jnp
from jax import lax
from jax.experimental import pallas as pl
from jax.experimental.pallas import tpu as pltpu
from jax.sharding import PartitionSpec as P

KP = 12
MESH = pl.DeviceIdType.MESH
TAB = 16
LAG = 2
VMEM_LIMIT = 251 * 256 * 1024


def partner(index, bit):
    return index + bit - 2 * bit * ((index // bit) % 2)


def bits_of(size):
    bits = []
    while size > 1:
        size //= 2
        bits.append(size)
    return bits


def moved(index, e, bits):
    for bit in bits:
        if e & bit:
            index = partner(index, bit)
    return index


def lower_bits(e, bits):
    return [n for n, bit in enumerate(bits) if e == 0 or bit < (e & -e)]


def placed(tabs, want, parts):
    outs = [jnp.zeros_like(part) for part in parts[0]]
    for tab, part in zip(tabs, parts):
        mask = tab == want
        outs = [jnp.where(mask, new, old) for new, old in zip(part, outs)]
    return outs


def spread_rows(tab, slots):
    return [jnp.broadcast_to(tab[s : s + 1, :], tab.shape) for s in range(slots)]


def kernel(dims, lpos, lcnt, rpos, rcnt, lhbm, rhbm, out_ref, lblk, rblk, lbuf, rbuf, ld, rd, insem, lsend, lrecv, rsend, rrecv):
    rows, cols, layers, rl, pg, cl, slots, side = dims
    half = side // 2
    width = 2 * side
    r, c, d = lax.axis_index("row"), lax.axis_index("col"), lax.axis_index("depth")
    lbits, rbits = bits_of(layers), bits_of(rows)
    chunks = pg * cl // 2
    me = c * layers + d
    parts_of = 2 if rl % 2 == 0 else 1
    pl_rows = rl // parts_of

    left_in = pltpu.make_async_copy(lhbm, lblk, insem.at[chunks])
    left_in.start()

    def right_in(chunk):
        at = pl.ds(2 * chunk, 2)
        return pltpu.make_async_copy(rhbm.at[at], rblk.at[at], insem.at[chunk])

    for chunk in range(chunks):
        right_in(chunk).start()

    lane = lax.broadcasted_iota(jnp.int32, (TAB, width), 1)
    line = lax.broadcasted_iota(jnp.int32, (TAB, width), 0)

    def shown(position, count, s):
        return jnp.where(s < count, position, KP)

    barrier = pltpu.get_barrier_semaphore()
    peers = [{"depth": partner(d, bit)} for bit in lbits] + [{"row": partner(r, bit)} for bit in rbits]
    if cols > 1:
        peers += [{"col": lax.rem(c + 1, cols)}, {"col": lax.rem(c + cols - 1, cols)}]
    for peer in peers:
        pl.semaphore_signal(barrier, inc=1, device_id=peer, device_id_type=MESH)

    left_in.wait()

    def pack_left(i, carry):
        tab = jnp.full((TAB, width), KP, jnp.int32)
        for s in range(slots):
            x = lblk[i, s]
            lbuf[me, i, s * half : (s + 1) * half, :] = jnp.concatenate([x[:half], x[half:]], axis=1)
            tab = jnp.where(line == s, shown(lpos[i, s], lcnt[i], s), tab)
        lbuf[me, i, slots * half : slots * half + TAB, :] = tab.astype(jnp.float32).astype(jnp.bfloat16)
        return carry

    lax.fori_loop(0, rl, pack_left, 0)
    pl.semaphore_wait(barrier, len(peers))

    def left_copy(way, owner, h, device):
        piece = lbuf.at[owner, pl.ds(h * pl_rows, pl_rows)]
        return pltpu.make_async_remote_copy(
            src_ref=piece,
            dst_ref=piece,
            send_sem=lsend.at[way, owner, h],
            recv_sem=lrecv.at[owner, h],
            device_id=device,
            device_id_type=MESH,
        )

    def left_sends(t, h, side_of, e, act):
        src = c + t if side_of else c - t
        owner = src * layers + moved(d, e, lbits)
        if e == 0:
            if side_of == 0:
                @pl.when(c + 1 < cols)
                def _():
                    act(left_copy(0, owner, h, {"col": c + 1}))

            def to_lower():
                act(left_copy(1, owner, h, {"col": c - 1}))

            if side_of == 1:
                pl.when(c > 0)(to_lower)
            else:
                pl.when((c > 0) & (t == 0))(to_lower)
        for n in lower_bits(e, lbits):
            act(left_copy(2 + n, owner, h, {"depth": partner(d, lbits[n])}))

    def valid(t, side_of):
        if side_of:
            return (t > 0) & (c + t < cols)
        return (t >= 0) & (c - t >= 0)

    for h in range(parts_of):
        left_sends(0, h, 0, 0, lambda copy: copy.start())

    def right_copy(n, owner, chunk):
        return pltpu.make_async_remote_copy(
            src_ref=rbuf.at[owner, chunk],
            dst_ref=rbuf.at[owner, chunk],
            send_sem=rsend.at[n, owner, chunk],
            recv_sem=rrecv.at[owner, chunk],
            device_id={"row": partner(r, rbits[n])},
            device_id_type=MESH,
        )

    def pack_right(chunk, carry):
        right_in(chunk).wait()
        tab = jnp.full((TAB, width), KP, jnp.int32)
        g, j = chunk // (cl // 2), 2 * (chunk % (cl // 2))
        for s in range(slots):
            first = shown(rpos[s, g, j], rcnt[g, j], s)
            second = shown(rpos[s, g, j + 1], rcnt[g, j + 1], s)
            tab = jnp.where(line == s, jnp.where(lane < side, first, second), tab)
            rbuf[r, chunk, s * side : (s + 1) * side, :] = jnp.concatenate(
                [rblk[2 * chunk, s], rblk[2 * chunk + 1, s]], axis=1
            )
        rbuf[r, chunk, slots * side : slots * side + TAB, :] = tab.astype(jnp.float32).astype(jnp.bfloat16)
        for n in lower_bits(0, rbits):
            right_copy(n, r, chunk).start()
        return carry

    lax.fori_loop(0, chunks, pack_right, 0)

    def place_right(owner, chunk):
        g = owner * pg + chunk // (cl // 2)
        lanes = pl.ds(pl.multiple_of((chunk % (cl // 2)) * width, width), width)
        tabs = spread_rows(rbuf[owner, chunk, slots * side : slots * side + TAB, :], slots)
        for v in range(side // TAB):
            parts = [(rbuf[owner, chunk, s * side + v * TAB : s * side + (v + 1) * TAB, :],) for s in range(slots)]
            for p in range(KP):
                (block,) = placed(tabs, jnp.asarray(p, jnp.bfloat16), parts)
                rd[pl.ds(pl.multiple_of((g * KP + p) * side + v * TAB, TAB), TAB), lanes] = block

    upper = (lane >= side).astype(jnp.float32).astype(jnp.bfloat16)

    def place_left(src, layer, h):
        owner = src * layers + layer

        def one(i, carry):
            base = (layer * rl + i) * side
            tabs = spread_rows(lbuf[owner, i, slots * half : slots * half + TAB, :], slots)
            for v in range(half // TAB):
                parts = []
                for s in range(slots):
                    x = lbuf[owner, i, s * half + v * TAB : s * half + (v + 1) * TAB, :]
                    lo, hi = x[:, :side], x[:, side:]
                    parts.append((jnp.concatenate([lo, lo], axis=1), jnp.concatenate([hi, hi], axis=1)))
                for q in range(KP // 2):
                    top, bottom = placed(tabs, upper + jnp.asarray(2 * q, jnp.bfloat16), parts)
                    lanes = pl.ds(pl.multiple_of((src * (KP // 2) + q) * width, width), width)
                    ld[pl.ds(pl.multiple_of(base + v * TAB, TAB), TAB), lanes] = top
                    ld[pl.ds(pl.multiple_of(base + half + v * TAB, TAB), TAB), lanes] = bottom
            return carry

        lax.fori_loop(h * pl_rows, (h + 1) * pl_rows, one, 0)

    def own_right(chunk, carry):
        place_right(r, chunk)
        return carry

    lax.fori_loop(0, chunks, own_right, 0)

    order = sorted(range(layers), key=lambda e: (e.bit_count(), -e))
    last = max(e.bit_count() for e in order)

    def left_step(u, carry):
        t, h = u // parts_of, u % parts_of
        for e in order:
            lag = e.bit_count()
            for side_of in (0, 1):
                tt = t - lag

                @pl.when(valid(tt, side_of) & (tt < cols))
                def _(tt=tt, e=e, side_of=side_of):
                    src = c + tt if side_of else c - tt
                    layer = moved(d, e, lbits)

                    def arrive():
                        left_copy(0, src * layers + layer, h, {"depth": partner(d, 1)}).wait_recv()
                        left_sends(tt, h, side_of, e, lambda copy: copy.start())

                    if e == 0:
                        pl.when(tt > 0)(arrive)
                    else:
                        arrive()
                    place_left(src, layer, h)
        return carry

    def right_arrive(e, chunk):
        owner = moved(r, e, rbits)
        right_copy(0, owner, chunk).wait_recv()
        for n in lower_bits(e, rbits):
            right_copy(n, owner, chunk).start()
        place_right(owner, chunk)

    arrivals = sorted(range(1, rows), key=lambda e: (e.bit_count(), -e))
    steps = (cols + last - 1) * parts_of
    paired = rows == 2 and cols > 1

    def share(u):
        return jnp.clip(chunks * (u - LAG) // (steps - 1 - LAG), 0, chunks)

    def both_step(u, carry):
        left_step(u, carry)
        if paired:

            def one(chunk, carry):
                right_arrive(1, chunk)
                return carry

            lax.fori_loop(share(u - 1), share(u), one, 0)
        return carry

    lax.fori_loop(0, steps, both_step, 0)
    if not paired:
        for e in arrivals:

            def one(chunk, carry, e=e):
                right_arrive(e, chunk)
                return carry

            lax.fori_loop(0, chunks, one, 0)

    tile = rl * side

    def multiply(layer):
        at = pl.ds(pl.multiple_of(layer * tile, tile), tile)
        out_ref[at, :] = jnp.dot(ld[at, :], rd[...], preferred_element_type=jnp.float32).astype(jnp.bfloat16)

    early = [e for e in order if e.bit_count() < last or last == 0]
    late = [e for e in order if e not in early]

    def multiply_all(group):
        def one(n, carry):
            multiply(lax.rem(d + n, layers))
            return carry

        if len(group) == layers:
            lax.fori_loop(0, layers, one, 0)
        else:
            first = moved(d, late[0], lbits) if late else d

            def other(n, carry):
                multiply(lax.rem(first + 1 + n, layers))
                return carry

            if group is early:
                lax.fori_loop(0, layers - 1, other, 0)
            else:
                multiply(first)

    multiply_all(early)
    lax.fori_loop(steps, steps + parts_of, left_step, 0)
    if late:
        multiply_all(late)

    def left_done(u, carry):
        t, h = u // parts_of, u % parts_of
        for e in range(layers):
            for side_of in (0, 1):

                @pl.when(valid(t, side_of))
                def _(e=e, side_of=side_of):
                    left_sends(t, h, side_of, e, lambda copy: copy.wait_send())

        return carry

    lax.fori_loop(0, cols * parts_of, left_done, 0)
    for e in range(rows):
        owner = moved(r, e, rbits)

        def right_done(chunk, carry, owner=owner, e=e):
            for n in lower_bits(e, rbits):
                right_copy(n, owner, chunk).wait_send()
            return carry

        lax.fori_loop(0, chunks, right_done, 0)


def on_device(row_blocks, row_positions, row_counts, col_blocks, col_positions, col_counts):
    rows, cols, layers = lax.axis_size("row"), lax.axis_size("col"), lax.axis_size("depth")
    rl, _, slots, side, _ = row_blocks.shape
    pg, cl = col_blocks.shape[:2]
    panels = pg * rows
    chunks = pg * cl // 2
    m, n, k = layers * rl * side, cl * side, panels * KP * side
    width = 2 * side
    vmem = pl.BlockSpec(memory_space=pltpu.VMEM)
    smem = pl.BlockSpec(memory_space=pltpu.SMEM)
    hbm = pl.BlockSpec(memory_space=pltpu.HBM)
    return pl.pallas_call(
        functools.partial(kernel, (rows, cols, layers, rl, pg, cl, slots, side)),
        out_shape=jax.ShapeDtypeStruct((m, n), jnp.bfloat16),
        in_specs=[smem] * 4 + [hbm] * 2,
        out_specs=vmem,
        scratch_shapes=[
            pltpu.VMEM((rl, slots, side, side), jnp.bfloat16),
            pltpu.VMEM((pg * cl, slots, side, side), jnp.bfloat16),
            pltpu.VMEM((cols * layers, rl, slots * side // 2 + TAB, width), jnp.bfloat16),
            pltpu.VMEM((rows, chunks, slots * side + TAB, width), jnp.bfloat16),
            pltpu.VMEM((m, k), jnp.bfloat16),
            pltpu.VMEM((k, n), jnp.bfloat16),
            pltpu.SemaphoreType.DMA((chunks + 1,)),
            pltpu.SemaphoreType.DMA((2 + len(bits_of(layers)), cols * layers, 2)),
            pltpu.SemaphoreType.DMA((cols * layers, 2)),
            pltpu.SemaphoreType.DMA((len(bits_of(rows)), rows, chunks)),
            pltpu.SemaphoreType.DMA((rows, chunks)),
        ],
        compiler_params=pltpu.CompilerParams(
            collective_id=0, has_side_effects=True, vmem_limit_bytes=VMEM_LIMIT
        ),
        cost_estimate=pl.CostEstimate(flops=2 * m * n * k, bytes_accessed=2 * m * n, transcendentals=0),
    )(
        row_positions[:, 0],
        row_counts[:, 0],
        col_positions.transpose(2, 0, 1),
        col_counts,
        row_blocks[:, 0],
        col_blocks.reshape(pg * cl, slots, side, side),
    )


def solution(mesh):
    in_specs = (
        P(("row", "depth"), "col", None, None, None),
        P(("row", "depth"), "col", None),
        P(("row", "depth"), "col"),
        P("row", ("col", "depth"), None, None, None),
        P("row", ("col", "depth"), None),
        P("row", ("col", "depth")),
    )
    return jax.shard_map(
        on_device, mesh=mesh, in_specs=in_specs, out_specs=P("row", ("col", "depth")), check_vma=False
    )
```

```python
import functools

import jax
import jax.numpy as jnp
from jax import lax
from jax.experimental import pallas as pl
from jax.experimental.pallas import tpu as pltpu
from jax.sharding import PartitionSpec as P

KP = 12
MESH = pl.DeviceIdType.MESH
TAB = 16
LAG = 2
VMEM_LIMIT = 251 * 256 * 1024


def partner(index, bit):
    return index + bit - 2 * bit * ((index // bit) % 2)


def bits_of(size):
    bits = []
    while size > 1:
        size //= 2
        bits.append(size)
    return bits


def moved(index, e, bits):
    for bit in bits:
        if e & bit:
            index = partner(index, bit)
    return index


def lower_bits(e, bits):
    return [n for n, bit in enumerate(bits) if e == 0 or bit < (e & -e)]


def placed(tabs, want, parts):
    outs = [jnp.zeros_like(part) for part in parts[0]]
    for tab, part in zip(tabs, parts):
        mask = tab == want
        outs = [jnp.where(mask, new, old) for new, old in zip(part, outs)]
    return outs


def spread_rows(tab, slots):
    return [jnp.broadcast_to(tab[s : s + 1, :], tab.shape) for s in range(slots)]


def kernel(dims, lpos, lcnt, rpos, rcnt, lhbm, rhbm, out_ref, lblk, rblk, lbuf, rbuf, ld, rd, acc, insem, lsend, lrecv, rsend, rrecv):
    rows, cols, layers, rl, pg, cl, slots, side = dims
    half = side // 2
    width = 2 * side
    r, c, d = lax.axis_index("row"), lax.axis_index("col"), lax.axis_index("depth")
    lbits, rbits = bits_of(layers), bits_of(rows)
    chunks = pg * cl // 2
    me = c * layers + d
    parts_of = 2
    pl_rows = rl // parts_of
    body = slots * half

    left_in = pltpu.make_async_copy(lhbm, lblk, insem.at[chunks])
    left_in.start()

    def right_in(chunk):
        at = pl.ds(2 * chunk, 2)
        return pltpu.make_async_copy(rhbm.at[at], rblk.at[at], insem.at[chunk])

    for chunk in range(chunks):
        right_in(chunk).start()

    lane = lax.broadcasted_iota(jnp.int32, (TAB, width), 1)
    line = lax.broadcasted_iota(jnp.int32, (TAB, width), 0)

    def shown(position, count, s):
        return jnp.where(s < count, position, KP)

    barrier = pltpu.get_barrier_semaphore()
    peers = [{"depth": partner(d, bit)} for bit in lbits] + [{"row": partner(r, bit)} for bit in rbits]
    if cols > 1:
        peers += [{"col": lax.rem(c + 1, cols)}, {"col": lax.rem(c + cols - 1, cols)}]
    for peer in peers:
        pl.semaphore_signal(barrier, inc=1, device_id=peer, device_id_type=MESH)

    left_in.wait()

    def pack_left(h, carry):
        tab = jnp.full((TAB, width), KP, jnp.int32)
        for i2 in range(pl_rows):
            i = h * pl_rows + i2
            for s in range(slots):
                x = lblk[i, s]
                at = i2 * body + s * half
                lbuf[me, h, at : at + half, :] = jnp.concatenate([x[:half], x[half:]], axis=1)
                tab = jnp.where(line == i2 * slots + s, shown(lpos[i, s], lcnt[i], s), tab)
        lbuf[me, h, pl_rows * body :, :] = tab.astype(jnp.float32).astype(jnp.bfloat16)
        return carry

    lax.fori_loop(0, parts_of, pack_left, 0)
    pl.semaphore_wait(barrier, len(peers))

    def left_copy(way, owner, h, device):
        piece = lbuf.at[owner, h]
        return pltpu.make_async_remote_copy(
            src_ref=piece,
            dst_ref=piece,
            send_sem=lsend.at[way, owner, h],
            recv_sem=lrecv.at[owner, h],
            device_id=device,
            device_id_type=MESH,
        )

    def left_sends(t, h, side_of, e, act):
        src = c + t if side_of else c - t
        owner = src * layers + moved(d, e, lbits)
        if e == 0:
            if side_of == 0:
                @pl.when(c + 1 < cols)
                def _():
                    act(left_copy(0, owner, h, {"col": c + 1}))

            def to_lower():
                act(left_copy(1, owner, h, {"col": c - 1}))

            if side_of == 1:
                pl.when(c > 0)(to_lower)
            else:
                pl.when((c > 0) & (t == 0))(to_lower)
        for n in lower_bits(e, lbits):
            act(left_copy(2 + n, owner, h, {"depth": partner(d, lbits[n])}))

    def valid(t, side_of):
        if side_of:
            return (t > 0) & (c + t < cols)
        return (t >= 0) & (c - t >= 0)

    for h in range(parts_of):
        left_sends(0, h, 0, 0, lambda copy: copy.start())

    def right_copy(n, owner, chunk):
        return pltpu.make_async_remote_copy(
            src_ref=rbuf.at[owner, chunk],
            dst_ref=rbuf.at[owner, chunk],
            send_sem=rsend.at[n, owner, chunk],
            recv_sem=rrecv.at[owner, chunk],
            device_id={"row": partner(r, rbits[n])},
            device_id_type=MESH,
        )

    def pack_right(chunk, carry):
        right_in(chunk).wait()
        tab = jnp.full((TAB, width), KP, jnp.int32)
        g, j = chunk // (cl // 2), 2 * (chunk % (cl // 2))
        for s in range(slots):
            first = shown(rpos[s, g, j], rcnt[g, j], s)
            second = shown(rpos[s, g, j + 1], rcnt[g, j + 1], s)
            tab = jnp.where(line == s, jnp.where(lane < side, first, second), tab)
            rbuf[r, chunk, s * side : (s + 1) * side, :] = jnp.concatenate(
                [rblk[2 * chunk, s], rblk[2 * chunk + 1, s]], axis=1
            )
        rbuf[r, chunk, slots * side : slots * side + TAB, :] = tab.astype(jnp.float32).astype(jnp.bfloat16)
        for n in lower_bits(0, rbits):
            right_copy(n, r, chunk).start()
        return carry

    lax.fori_loop(0, chunks, pack_right, 0)

    def place_right(owner, chunk):
        g = owner * pg + chunk // (cl // 2)
        lanes = pl.ds(pl.multiple_of((chunk % (cl // 2)) * width, width), width)
        tabs = spread_rows(rbuf[owner, chunk, slots * side : slots * side + TAB, :], slots)
        for v in range(side // TAB):
            parts = [(rbuf[owner, chunk, s * side + v * TAB : s * side + (v + 1) * TAB, :],) for s in range(slots)]
            for p in range(KP):
                (block,) = placed(tabs, jnp.asarray(p, jnp.bfloat16), parts)
                rd[pl.ds(pl.multiple_of((g * KP + p) * side + v * TAB, TAB), TAB), lanes] = block

    upper = (lane >= side).astype(jnp.float32).astype(jnp.bfloat16)

    def place_left(src, layer, h):
        owner = src * layers + layer

        tabs = spread_rows(lbuf[owner, h, pl_rows * body :, :], pl_rows * slots)
        for i2 in range(pl_rows):
            base = (layer * rl + h * pl_rows + i2) * side
            mine = tabs[i2 * slots : (i2 + 1) * slots]
            for v in range(half // TAB):
                parts = []
                for s in range(slots):
                    at = i2 * body + s * half + v * TAB
                    x = lbuf[owner, h, at : at + TAB, :]
                    lo, hi = x[:, :side], x[:, side:]
                    parts.append((jnp.concatenate([lo, lo], axis=1), jnp.concatenate([hi, hi], axis=1)))
                for q in range(KP // 2):
                    top, bottom = placed(mine, upper + jnp.asarray(2 * q, jnp.bfloat16), parts)
                    lanes = pl.ds(pl.multiple_of((src * (KP // 2) + q) * width, width), width)
                    ld[pl.ds(pl.multiple_of(base + v * TAB, TAB), TAB), lanes] = top
                    ld[pl.ds(pl.multiple_of(base + half + v * TAB, TAB), TAB), lanes] = bottom

    def own_right(chunk, carry):
        place_right(r, chunk)
        return carry

    lax.fori_loop(0, chunks, own_right, 0)

    tile = rl * side
    paired = rows == 2 and cols > 1
    if paired:
        acc[...] = jnp.zeros_like(acc)

    order = sorted(range(layers), key=lambda e: (e.bit_count(), -e))
    last = max(e.bit_count() for e in order)

    def left_step(u, carry):
        t, h = u // parts_of, u % parts_of
        for e in order:
            lag = e.bit_count()
            for side_of in (0, 1):
                tt = t - lag

                @pl.when(valid(tt, side_of) & (tt < cols))
                def _(tt=tt, e=e, side_of=side_of):
                    src = c + tt if side_of else c - tt
                    layer = moved(d, e, lbits)

                    def arrive():
                        left_copy(0, src * layers + layer, h, {"depth": partner(d, 1)}).wait_recv()
                        left_sends(tt, h, side_of, e, lambda copy: copy.start())

                    if e == 0:
                        pl.when(tt > 0)(arrive)
                    else:
                        arrive()
                    place_left(src, layer, h)
                    if paired:

                        @pl.when((src // pg == r) & (h == parts_of - 1))
                        def _():
                            at = pl.ds(pl.multiple_of(layer * tile, tile), tile)
                            inner = pl.ds(pl.multiple_of(src * KP * side, KP * side), KP * side)
                            acc[at, :] += jnp.dot(ld[at, inner], rd[inner, :], preferred_element_type=jnp.float32)

        return carry

    def right_arrive(e, chunk):
        owner = moved(r, e, rbits)
        right_copy(0, owner, chunk).wait_recv()
        for n in lower_bits(e, rbits):
            right_copy(n, owner, chunk).start()
        place_right(owner, chunk)

    arrivals = sorted(range(1, rows), key=lambda e: (e.bit_count(), -e))
    steps = (cols + last - 1) * parts_of

    def share(u):
        return jnp.clip(chunks * (u - LAG) // (steps - 1 - LAG), 0, chunks)

    def both_step(u, carry):
        left_step(u, carry)
        if paired:

            def one(chunk, carry):
                right_arrive(1, chunk)
                return carry

            lax.fori_loop(share(u - 1), share(u), one, 0)
        return carry

    lax.fori_loop(0, steps, both_step, 0)
    if not paired:
        for e in arrivals:

            def one(chunk, carry, e=e):
                right_arrive(e, chunk)
                return carry

            lax.fori_loop(0, chunks, one, 0)

    def multiply(layer):
        at = pl.ds(pl.multiple_of(layer * tile, tile), tile)
        if paired:
            size = pg * KP * side
            inner = pl.ds(pl.multiple_of((1 - r) * size, size), size)
            total = acc[at, :] + jnp.dot(ld[at, inner], rd[inner, :], preferred_element_type=jnp.float32)
        else:
            total = jnp.dot(ld[at, :], rd[...], preferred_element_type=jnp.float32)
        out_ref[at, :] = total.astype(jnp.bfloat16)

    early = [e for e in order if e.bit_count() < last or last == 0]
    late = [e for e in order if e not in early]

    def multiply_all(group):
        def one(n, carry):
            multiply(lax.rem(d + n, layers))
            return carry

        if len(group) == layers:
            lax.fori_loop(0, layers, one, 0)
        else:
            first = moved(d, late[0], lbits) if late else d

            def other(n, carry):
                multiply(lax.rem(first + 1 + n, layers))
                return carry

            if group is early:
                lax.fori_loop(0, layers - 1, other, 0)
            else:
                multiply(first)

    multiply_all(early)
    lax.fori_loop(steps, steps + parts_of, left_step, 0)
    if late:
        multiply_all(late)

    def left_done(u, carry):
        t, h = u // parts_of, u % parts_of
        for e in range(layers):
            for side_of in (0, 1):

                @pl.when(valid(t, side_of))
                def _(e=e, side_of=side_of):
                    left_sends(t, h, side_of, e, lambda copy: copy.wait_send())

        return carry

    lax.fori_loop(0, cols * parts_of, left_done, 0)
    for e in range(rows):
        owner = moved(r, e, rbits)

        def right_done(chunk, carry, owner=owner, e=e):
            for n in lower_bits(e, rbits):
                right_copy(n, owner, chunk).wait_send()
            return carry

        lax.fori_loop(0, chunks, right_done, 0)


def on_device(row_blocks, row_positions, row_counts, col_blocks, col_positions, col_counts):
    rows, cols, layers = lax.axis_size("row"), lax.axis_size("col"), lax.axis_size("depth")
    rl, _, slots, side, _ = row_blocks.shape
    pg, cl = col_blocks.shape[:2]
    panels = pg * rows
    chunks = pg * cl // 2
    m, n, k = layers * rl * side, cl * side, panels * KP * side
    width = 2 * side
    vmem = pl.BlockSpec(memory_space=pltpu.VMEM)
    smem = pl.BlockSpec(memory_space=pltpu.SMEM)
    hbm = pl.BlockSpec(memory_space=pltpu.HBM)
    return pl.pallas_call(
        functools.partial(kernel, (rows, cols, layers, rl, pg, cl, slots, side)),
        out_shape=jax.ShapeDtypeStruct((m, n), jnp.bfloat16),
        in_specs=[smem] * 4 + [hbm] * 2,
        out_specs=vmem,
        scratch_shapes=[
            pltpu.VMEM((rl, slots, side, side), jnp.bfloat16),
            pltpu.VMEM((pg * cl, slots, side, side), jnp.bfloat16),
            pltpu.VMEM((cols * layers, 2, rl // 2 * slots * side // 2 + TAB, width), jnp.bfloat16),
            pltpu.VMEM((rows, chunks, slots * side + TAB, width), jnp.bfloat16),
            pltpu.VMEM((m, k), jnp.bfloat16),
            pltpu.VMEM((k, n), jnp.bfloat16),
            pltpu.VMEM((m if rows == 2 else 8, n), jnp.float32),
            pltpu.SemaphoreType.DMA((chunks + 1,)),
            pltpu.SemaphoreType.DMA((2 + len(bits_of(layers)), cols * layers, 2)),
            pltpu.SemaphoreType.DMA((cols * layers, 2)),
            pltpu.SemaphoreType.DMA((len(bits_of(rows)), rows, chunks)),
            pltpu.SemaphoreType.DMA((rows, chunks)),
        ],
        compiler_params=pltpu.CompilerParams(
            collective_id=0, has_side_effects=True, vmem_limit_bytes=VMEM_LIMIT
        ),
        cost_estimate=pl.CostEstimate(flops=2 * m * n * k, bytes_accessed=2 * m * n, transcendentals=0),
    )(
        row_positions[:, 0],
        row_counts[:, 0],
        col_positions.transpose(2, 0, 1),
        col_counts,
        row_blocks[:, 0],
        col_blocks.reshape(pg * cl, slots, side, side),
    )


def solution(mesh):
    in_specs = (
        P(("row", "depth"), "col", None, None, None),
        P(("row", "depth"), "col", None),
        P(("row", "depth"), "col"),
        P("row", ("col", "depth"), None, None, None),
        P("row", ("col", "depth"), None),
        P("row", ("col", "depth")),
    )
    return jax.shard_map(
        on_device, mesh=mesh, in_specs=in_specs, out_specs=P("row", ("col", "depth")), check_vma=False
    )
```
